32 devices in a mesh: wide: 8 (over z, x), narrow: 4 (over y, core).
Axes of the slice: x: 2, y: 2, z: 4, core: 2. Of those that a mesh axis runs over, the one named last changes fastest.
Arguments:
- attn_heads: bfloat16 [1024, 1536], P('wide', 'narrow'), may hold values from -6 to 6
- w_out: bfloat16 [1536, 1536], P('narrow'), may hold values from -0.21875 to 0.21875
- residual: bfloat16 [1024, 1536], P('wide', 'narrow'), may hold values from -6 to 6
- norm_gain: float32 [1536], replicated, may hold values from 0.1 to 1.9
- route_ids: int32 [1024, 4], P('wide'), may hold values from 0 to 31, all different within a row; in each aligned block of 128 rows (0 to 127, 128 to 255, ...) at most 32 rows name the same one
- route_weight: float32 [1024, 4], P('wide'), may hold values from 0.1 to 1
- row_order: int32 [1024], P('wide'), may hold values from 0 to 1023, as said below
- slot_expert: int32 [64], replicated, may hold values from 0 to 31, as said below
- w_in: bfloat16 [64, 2, 768, 1536], P('wide', None, 'narrow')
- w_down: bfloat16 [64, 768, 1536], P('wide', 'narrow')
Outputs:
- block_out: bfloat16 [1024, 1536], P('wide', 'narrow')
The draws below stay inside these ranges and needn't reach their ends.
Inputs may be any that keep to these rules, and one draw needn't show every extreme that they name: `route_ids`: each row names 4 different experts; among the 128 rows of one index of wide no expert is named more than 32 times. `row_order`: A permutation of the rows; of the 128 rows of each index of wide, exactly 16 have their initial position among the rows of each index of wide. `slot_expert`: every expert is held by one or more slots; slots holding the same expert hold equal w_in and w_down.
All inputs are finite; a program needn't handle non-finite values.
Results may differ from the reference program's by a relative error of at most 0.017.
Values may be sent and summed in bfloat16 or wider, within the bound.
A program may use at most 128 MiB of HBM per device.

```python
import math
import jax
import jax.numpy as jnp
import numpy as np
from jax import lax

D = 1536
HID = 768
EXPERTS = 32
TOP = 4
TOK_DEV = 128
F = 1536
TOKENS = 1024
CAP = 32
SLOTS = 64
N_WIDE = 8
N_NARROW = 4


def slot_table(key):
    first = jax.random.permutation(jax.random.fold_in(key, 11), EXPERTS).astype(jnp.int32)
    extra = jax.random.randint(jax.random.fold_in(key, 12), (SLOTS - EXPERTS,), 0, EXPERTS).astype(jnp.int32)
    joined = jnp.concatenate([first, extra])
    return jax.random.permutation(jax.random.fold_in(key, 13), joined).astype(jnp.int32)


def draw_slot_expert(key, part):
    return slot_table(key)


def draw_w_in(key, part):
    table = slot_table(key)
    inner = jax.random.fold_in(key, 21)
    values = jax.random.normal(inner, (EXPERTS, 2, HID, D), jnp.float32)
    return (values * D ** (-0.5))[table].astype(jnp.bfloat16)


def draw_w_down(key, part):
    table = slot_table(key)
    inner = jax.random.fold_in(key, 22)
    values = jax.random.normal(inner, (EXPERTS, HID, D), jnp.float32)
    return (values * HID ** (-0.5))[table].astype(jnp.bfloat16)


def draw_row_order(key, part):
    blocks = TOKENS // TOK_DEV
    pair_rows = TOK_DEV // blocks
    source_keys = jax.random.split(jax.random.fold_in(key, 31), blocks)
    target_keys = jax.random.split(jax.random.fold_in(key, 32), blocks)
    source_perm = jax.vmap(lambda k: jax.random.permutation(k, TOK_DEV))(source_keys).astype(jnp.int32)
    target_perm = jax.vmap(lambda k: jax.random.permutation(k, TOK_DEV))(target_keys).astype(jnp.int32)
    src_index = jnp.arange(blocks, dtype=jnp.int32)[:, None, None]
    dst_index = jnp.arange(blocks, dtype=jnp.int32)[None, :, None]
    pair_index = jnp.arange(pair_rows, dtype=jnp.int32)[None, None, :]
    processed = src_index * TOK_DEV + source_perm[src_index, dst_index * pair_rows + pair_index]
    initial = dst_index * TOK_DEV + target_perm[dst_index, src_index * pair_rows + pair_index]
    return jnp.zeros((TOKENS,), jnp.int32).at[processed.reshape(-1)].set(initial.reshape(-1))


def with_spikes(entries, key, source, target, parts, factor):
    def block_of(dim):
        return (jnp.arange(entries.shape[dim]) // (entries.shape[dim] // parts)).reshape((-1,) + (1,) * (entries.ndim - 1 - dim))

    one_side = jax.random.permutation(key, parts)[block_of(target)]
    other_side = (block_of(target) + parts // 2) % parts
    return jnp.where((block_of(source) == one_side) | (block_of(source) == other_side), factor * entries, entries)


def block_scale(own_key, extent, shards, smallest, largest):
    def one(position, blocks):
        heights = jax.random.uniform(jax.random.fold_in(jax.random.fold_in(own_key, 6), position), (blocks,), jnp.float32, smallest / len(shards), largest / len(shards))
        return jnp.repeat(jnp.exp(heights), extent[position] // blocks).reshape((-1,) + (1,) * (len(extent) - position - 1))

    level = one(*shards[0])
    for cut in shards[1:]:
        level = level * one(*cut)
    return level


def assign_block(key, own, number, rows, amount, top, reach, lean):
    ranking = jax.random.permutation(key, amount)
    crowded, ordinary = shares(amount, rows * top, reach, lean, True), shares(amount, rows * top, reach, lean, False)
    places = jnp.arange(amount)

    def named(sizes, turn):
        used = int((sizes > 0).sum())
        fixed = max(1, used // 4)
        shifted = fixed + (places - fixed + turn * (used - fixed)) % max(1, amount - fixed)
        return jnp.zeros((amount,), jnp.int32).at[ranking[jnp.where(places < fixed, places, shifted)]].set(jnp.asarray(sizes, jnp.int32))

    sizes = jnp.where(number % 4 == 0, named(crowded, number // 4), named(ordinary, number - number // 4 - 1))
    mixed = jax.random.permutation(jax.random.fold_in(own, 3), amount)
    source_of, sink = mixed[0:amount // 2 * 2:2], mixed[1:amount // 2 * 2:2]
    margin = jnp.minimum(sizes[source_of] - 1, reach - sizes[sink]) // 2
    margin = jnp.where((source_of == ranking[0]) | (sink == ranking[0]) | (sizes[sink] == 0), 0, jnp.maximum(margin, 0))
    shifted = jax.random.randint(jax.random.fold_in(own, 4), (amount // 2,), 0, 1 << 20) % (margin + 1)
    sizes = sizes.at[source_of].add(-shifted).at[sink].add(shifted)
    members = jnp.searchsorted(jnp.cumsum(sizes), jnp.arange(rows * top), side="right").astype(jnp.int32)
    table = members.reshape(top, rows).T
    table = table[jax.random.permutation(jax.random.fold_in(own, 1), rows)]
    turn = jax.random.randint(jax.random.fold_in(own, 2), (rows, 1), 0, top)
    return jnp.take_along_axis(table, (jnp.arange(top)[None, :] + turn) % top, axis=1)


def shares(amount, total, reach, lean, full):
    loads = [(1 << 20) // math.isqrt(grade ** lean) + 1 for grade in range(1, amount + 1)]
    largest = reach if full else min(reach, max(-(-total // amount), total * loads[0] // sum(loads)))
    least = 1 if total - largest >= amount - 1 else 0
    counts, surplus = [largest] + [least] * (amount - 1), total - largest - least * (amount - 1)
    while surplus > 0:
        movable = [i for i in range(1, amount) if counts[i] < largest] or [i for i in range(1, amount) if counts[i] < reach]
        whole, remaining = sum([loads[i] for i in movable]), surplus
        for i in movable:
            more = min(reach - counts[i], max(1, remaining * loads[i] // whole), surplus)
            counts[i] = counts[i] + more
            surplus = surplus - more
    return np.array(counts)


def gaussian(stream_key, shape, spread, bound, cuts=(), held_as=jnp.bfloat16):
    level = block_scale(stream_key, shape, cuts, -0.22, 0.18) if cuts else 1.0
    array = jax.random.normal(stream_key, shape, jnp.float32) * spread * level
    return jnp.minimum(jnp.maximum(array, -bound), bound).astype(held_as)


def gaussian_with(rng, extent, scale, limit, cuts, heavy, kind=jnp.bfloat16):
    values = scale * jax.random.normal(rng, extent, jnp.float32)
    if cuts:
        values = values * block_scale(rng, extent, cuts, -0.22, 0.18)
    return jnp.clip(with_spikes(values, jax.random.fold_in(rng, 3), *heavy), -limit, limit).astype(kind)


def setup_inputs(seed: int = 0) -> dict:
    key_of = jax.random.split(jax.random.key(seed), 11)
    attn_heads = gaussian(key_of[0], (TOKENS, F), 1.0, 6.0, ((0, 8), (1, 4)))
    w_out = gaussian_with(key_of[1], (F, D), F ** -0.5, 0.21875, ((0, 4),), (0, 1, 4, 2.0))
    residual = gaussian(key_of[2], (TOKENS, D), 1.0, 6.0, ((0, 8), (1, 4)))
    norm_gain = jnp.clip(1.0 + 0.18 * jax.random.normal(key_of[3], (D,), jnp.float32), 0.1, 1.9)
    route_ids_keys = jax.random.split(jax.random.fold_in(key_of[4], 1), TOKENS // TOK_DEV)
    route_ids_turns = jax.random.permutation(jax.random.fold_in(key_of[4], 3), TOKENS // TOK_DEV)
    route_ids = jax.vmap(lambda own, number: assign_block(jax.random.fold_in(key_of[4], 2), own, number, TOK_DEV, EXPERTS, TOP, CAP, 2))(route_ids_keys, route_ids_turns).reshape((TOKENS, TOP))
    route_weight = jnp.clip(jnp.exp(math.log(1.0) - 2.3025851 * jax.random.uniform(key_of[5], (TOKENS, TOP), jnp.float32) ** block_scale(key_of[5], (TOKENS, TOP), ((0, 8),), -0.2, 0.2)), 0.1, 1.0)
    row_order = draw_row_order(jax.random.fold_in(key_of[10], 71), 0)
    slot_expert = draw_slot_expert(jax.random.fold_in(key_of[10], 71), 0)
    w_in = draw_w_in(jax.random.fold_in(key_of[10], 71), 0)
    w_down = draw_w_down(jax.random.fold_in(key_of[10], 71), 0)
    return {"attn_heads": attn_heads, "w_out": w_out, "residual": residual, "norm_gain": norm_gain, "route_ids": route_ids, "route_weight": route_weight, "row_order": row_order, "slot_expert": slot_expert, "w_in": w_in, "w_down": w_down}


def reference(attn_heads, w_out, residual, norm_gain, route_ids, route_weight, row_order, slot_expert, w_in, w_down):
    projected = jnp.dot(attn_heads, w_out, preferred_element_type=jnp.float32)
    hidden = (residual.astype(jnp.float32) + projected).astype(jnp.bfloat16)
    hidden_f = hidden.astype(jnp.float32)
    mean_sq = lax.optimization_barrier(jnp.mean(hidden_f * hidden_f, axis=1, keepdims=True))
    normed = (hidden_f * lax.rsqrt(mean_sq + 1e-06) * norm_gain).astype(jnp.bfloat16)
    flat_ids = route_ids.reshape(-1).astype(jnp.int32)
    total = flat_ids.shape[0]
    buffer_rows = N_WIDE * CAP
    quarter = HID // N_NARROW

    def one_expert(carry, expert):
        slot_index = jnp.argmax(slot_expert == expert).astype(jnp.int32)
        both = lax.dynamic_index_in_dim(w_in, slot_index, 0, keepdims=False)
        lower = lax.dynamic_index_in_dim(w_down, slot_index, 0, keepdims=False)
        picked = jnp.nonzero(flat_ids == expert, size=buffer_rows, fill_value=total)[0].astype(jnp.int32)
        source_rows = jnp.minimum(picked, total - 1) // TOP
        rows_in = normed[source_rows]
        gate = jnp.dot(rows_in, both[0].T, preferred_element_type=jnp.float32)
        upper = jnp.dot(rows_in, both[1].T, preferred_element_type=jnp.float32)
        active = (jax.nn.relu(gate) * upper).astype(jnp.bfloat16)
        summed = jnp.zeros((buffer_rows, D), jnp.float32)
        for quarter_index in range(N_NARROW):
            lo_edge = quarter_index * quarter
            piece = jnp.dot(active[:, lo_edge:lo_edge + quarter], lower[lo_edge:lo_edge + quarter], preferred_element_type=jnp.float32)
            summed = summed + lax.optimization_barrier(piece.astype(jnp.bfloat16)).astype(jnp.float32)
        carry = carry.at[picked].set(summed.astype(jnp.bfloat16), mode='drop')
        return (carry, None)
    expert_out, _ = lax.scan(one_expert, jnp.zeros((total, D), jnp.bfloat16), jnp.arange(EXPERTS, dtype=jnp.int32))
    weighted = route_weight[:, :, None] * expert_out.reshape(TOKENS, TOP, D).astype(jnp.float32)
    mixed = (hidden_f + lax.optimization_barrier(jnp.sum(weighted, axis=1))).astype(jnp.bfloat16)
    return jnp.zeros_like(mixed).at[row_order].set(mixed)
```

```python
import jax
import jax.numpy as jnp
from jax import lax
from jax.sharding import PartitionSpec as P


def local(
    attn_heads,
    w_out,
    residual,
    norm_gain,
    route_ids,
    route_weight,
    row_order,
    slot_expert,
    w_in,
    w_down,
):
    rows = residual.shape[0]
    wide = lax.axis_size("wide")
    me = lax.axis_index("wide")
    width_local = residual.shape[1]
    slot_local, _, hid, width = w_in.shape
    pair = rows // wide

    target = row_order // rows
    earlier = jnp.arange(rows)[None, :] < jnp.arange(rows)[:, None]
    rank = jnp.sum((target[:, None] == target[None, :]) & earlier, axis=1, dtype=jnp.int32)
    packed = target * pair + rank
    perm = packed[None, :] == jnp.arange(rows, dtype=jnp.int32)[:, None]
    order = perm.astype(jnp.bfloat16)
    meta = jnp.concatenate(
        [
            route_ids.astype(jnp.float32),
            route_weight,
            (row_order % rows).astype(jnp.float32)[:, None],
        ],
        axis=1,
    )
    meta = jnp.sum(jnp.where(perm[:, :, None], meta[None], 0.0), axis=1)
    metas = lax.all_gather(meta, "wide", axis=0, tiled=True)
    attn = jnp.dot(order, attn_heads, preferred_element_type=jnp.float32).astype(jnp.bfloat16)
    res = jnp.dot(order, residual, preferred_element_type=jnp.float32)

    partial_terms = jnp.dot(attn, w_out, preferred_element_type=jnp.float32)
    projected = lax.psum_scatter(
        partial_terms.astype(jnp.bfloat16), "narrow", scatter_dimension=1, tiled=True
    ).astype(jnp.float32)
    hidden = (res + projected).astype(jnp.bfloat16)
    column = lax.all_gather(hidden, "wide", axis=0, tiled=True)

    def regroup(x):
        return (
            x.reshape(wide, wide, pair, x.shape[1])
            .transpose(1, 0, 2, 3)
            .reshape(wide * rows, x.shape[1])
        )

    column = regroup(column)
    metas = regroup(metas)
    whole = lax.all_gather(column, "narrow", axis=1, tiled=True).astype(jnp.float32)
    mean_sq = jnp.mean(whole * whole, axis=1, keepdims=True)
    normed = (whole * lax.rsqrt(mean_sq + 1e-06) * norm_gain).astype(jnp.bfloat16)

    slots = slot_expert.shape[0]
    before = jnp.arange(slots)[None, :] < jnp.arange(slots)[:, None]
    repeated = jnp.any((slot_expert[:, None] == slot_expert[None, :]) & before, axis=1)
    used = jnp.where(repeated, -1, slot_expert)
    mine = lax.dynamic_slice_in_dim(used, me * slot_local, slot_local).astype(jnp.float32)
    ids, weights, places = metas[:, :4], metas[:, 4:8], metas[:, 8]
    coef = jnp.sum(
        jnp.where(ids[:, :, None] == mine[None, None, :], weights[:, :, None], 0.0), axis=1
    )

    gate = jnp.einsum("rd,shd->rsh", normed, w_in[:, 0], preferred_element_type=jnp.float32)
    up = jnp.einsum("rd,shd->rsh", normed, w_in[:, 1], preferred_element_type=jnp.float32)
    act = (jax.nn.relu(gate) * up * coef[:, :, None]).astype(jnp.bfloat16)
    lowered = jnp.dot(
        act.reshape(wide * rows, slot_local * hid),
        w_down.reshape(slot_local * hid, width),
        preferred_element_type=jnp.float32,
    ).astype(jnp.bfloat16)
    summed = lax.psum_scatter(lowered, "narrow", scatter_dimension=1, tiled=True)
    mixed = lax.psum_scatter(summed, "wide", scatter_dimension=0, tiled=True)
    base = lax.dynamic_slice_in_dim(column, me * rows, rows)
    mixed = (base.astype(jnp.float32) + mixed.astype(jnp.float32)).astype(jnp.bfloat16)
    place = lax.dynamic_slice_in_dim(places, me * rows, rows).astype(jnp.int32)
    back = (place[None, :] == jnp.arange(rows, dtype=jnp.int32)[:, None]).astype(jnp.bfloat16)
    return jnp.dot(back, mixed, preferred_element_type=jnp.float32).astype(jnp.bfloat16)


def solution(mesh):
    placed = (
        P("wide", "narrow"),
        P("narrow", None),
        P("wide", "narrow"),
        P(),
        P("wide", None),
        P("wide", None),
        P("wide"),
        P(),
        P("wide", None, "narrow", None),
        P("wide", "narrow", None),
    )
    return jax.shard_map(
        local, mesh=mesh, in_specs=placed, out_specs=P("wide", "narrow"), check_vma=False
    )
```

```python
import functools

import jax
import jax.numpy as jnp
from jax import lax
from jax.experimental import pallas as pl
from jax.experimental.pallas import tpu as pltpu
from jax.sharding import PartitionSpec as P

MESH = pl.DeviceIdType.MESH
NARROW = 4


def remote(src, dst, send_sem, recv_sem, wide_index, narrow_index):
    return pltpu.make_async_remote_copy(
        src_ref=src,
        dst_ref=dst,
        send_sem=send_sem,
        recv_sem=recv_sem,
        device_id=(wide_index, narrow_index),
        device_id_type=MESH,
    )


def greet(wide, me, col, others):
    barrier = pltpu.get_barrier_semaphore()

    def hello(j, carry):
        pl.semaphore_signal(
            barrier, inc=1, device_id=(lax.rem(me + j, wide), col), device_id_type=MESH
        )
        return carry

    lax.fori_loop(1, wide, hello, 0)
    for other in others:
        pl.semaphore_signal(barrier, inc=1, device_id=(me, other), device_id_type=MESH)
    pl.semaphore_wait(barrier, wide - 1 + len(others))


def gather_kernel(
    wide,
    attn_ref,
    w_ref,
    res_ref,
    out_ref,
    parts,
    got,
    mine,
    sum_send,
    sum_recv,
    local_sem,
    wide_send,
    wide_recv,
    y_send,
    y_recv,
    core_send,
    core_recv,
):
    me, col = lax.axis_index("wide"), lax.axis_index("narrow")
    half, core = col // 2, lax.rem(col, 2)
    y_col = (1 - half) * 2 + core
    core_col = half * 2 + 1 - core
    rows, cols = res_ref.shape
    greet(wide, me, col, [lax.rem(col + k, NARROW) for k in range(1, NARROW)])

    for p in range(NARROW):
        parts[p] = jnp.dot(
            attn_ref[...], w_ref[:, p * cols : (p + 1) * cols], preferred_element_type=jnp.float32
        ).astype(jnp.bfloat16)
    sums = []
    for k in range(1, NARROW):
        other = lax.rem(col + k, NARROW)
        copy = remote(
            parts.at[other], got.at[k - 1], sum_send.at[k - 1], sum_recv.at[k - 1], me, other
        )
        copy.start()
        sums.append(copy)
    total = res_ref[...] + parts[col].astype(jnp.float32)
    for k, copy in enumerate(sums):
        copy.wait_recv()
        total += got[k].astype(jnp.float32)
    mine[...] = total.astype(jnp.bfloat16)

    def block(source, column):
        return out_ref.at[
            pl.ds(pl.multiple_of(source * rows, rows), rows),
            pl.ds(pl.multiple_of(column * cols, cols), cols),
        ]

    def wide_copy(j):
        return remote(
            mine, block(me, col), wide_send.at[j], wide_recv.at[j], lax.rem(me + j, wide), col
        )

    def y_copy(j):
        b = block(lax.rem(me - j + wide, wide), col)
        return remote(b, b, y_send.at[j], y_recv.at[j], me, y_col)

    def core_copy(j, h):
        b = block(lax.rem(me - j + wide, wide), y_col if h else col)
        return remote(b, b, core_send.at[h, j], core_recv.at[h, j], me, core_col)

    def send_wide(j, carry):
        wide_copy(j).start()
        return carry

    lax.fori_loop(1, wide, send_wide, 0)
    keep = pltpu.make_async_copy(mine, block(me, col), local_sem)
    keep.start()
    keep.wait()
    y_copy(0).start()
    core_copy(0, 0).start()

    def forward(j, carry):
        wide_copy(j).wait_recv()
        y_copy(j).start()
        core_copy(j, 0).start()
        y_copy(j - 1).wait_recv()
        core_copy(j - 1, 1).start()
        return carry

    lax.fori_loop(1, wide, forward, 0)
    y_copy(wide - 1).wait_recv()
    core_copy(wide - 1, 1).start()

    def finish(j, carry):
        core_copy(j, 0).wait()
        core_copy(j, 1).wait()
        y_copy(j).wait_send()
        return carry

    lax.fori_loop(0, wide, finish, 0)

    def finish_wide(j, carry):
        wide_copy(j).wait_send()
        return carry

    lax.fori_loop(1, wide, finish_wide, 0)
    for copy in sums:
        copy.wait_send()


def gather_call(attn, w_out, res, wide):
    rows, cols = res.shape
    dma = pltpu.SemaphoreType.DMA
    vmem = pl.BlockSpec(memory_space=pltpu.VMEM)
    return pl.pallas_call(
        functools.partial(gather_kernel, wide),
        out_shape=jax.ShapeDtypeStruct((wide * rows, NARROW * cols), jnp.bfloat16),
        in_specs=[vmem] * 3,
        out_specs=pl.BlockSpec(memory_space=pl.ANY),
        scratch_shapes=[
            pltpu.VMEM((NARROW, rows, cols), jnp.bfloat16),
            pltpu.VMEM((NARROW - 1, rows, cols), jnp.bfloat16),
            pltpu.VMEM((rows, cols), jnp.bfloat16),
            dma((NARROW - 1,)),
            dma((NARROW - 1,)),
            dma,
            dma((wide,)),
            dma((wide,)),
            dma((wide,)),
            dma((wide,)),
            dma((2, wide)),
            dma((2, wide)),
        ],
        compiler_params=pltpu.CompilerParams(
            collective_id=0, has_side_effects=True, vmem_limit_bytes=32 * 2**20
        ),
    )(attn, w_out, res)


def scatter_kernel(
    wide,
    low_ref,
    base_ref,
    back_ref,
    out_ref,
    own,
    core_got,
    y_got,
    wide_got,
    local_sem,
    core_send,
    core_recv,
    y_send,
    y_recv,
    wide_send,
    wide_recv,
):
    me, col = lax.axis_index("wide"), lax.axis_index("narrow")
    half, core = col // 2, lax.rem(col, 2)
    y_col = (1 - half) * 2 + core
    core_col = half * 2 + 1 - core
    rows, cols = base_ref.shape
    greet(wide, me, col, [y_col, core_col])

    def target(j):
        return lax.rem(me + 1 + j, wide)

    def block(j, column):
        return low_ref.at[
            pl.ds(pl.multiple_of(target(j) * rows, rows), rows),
            pl.ds(pl.multiple_of(column * cols, cols), cols),
        ]

    def core_copy(j, h):
        return remote(
            block(j, h * 2 + 1 - core),
            core_got.at[j, h],
            core_send.at[h, j],
            core_recv.at[h, j],
            me,
            core_col,
        )

    def load(j, h):
        return pltpu.make_async_copy(block(j, h * 2 + core), own.at[j, h], local_sem.at[h, j])

    def y_copy(j):
        return remote(own.at[j, 1 - half], y_got.at[j], y_send.at[j], y_recv.at[j], me, y_col)

    def wide_copy(j):
        return remote(
            own.at[j, half], wide_got.at[j], wide_send.at[j], wide_recv.at[j], target(j), col
        )

    def begin(j, carry):
        for h in range(2):
            core_copy(j, h).start()
            load(j, h).start()
        return carry

    lax.fori_loop(0, wide, begin, 0)

    def add_core(j):
        for h in range(2):
            load(j, h).wait()
            core_copy(j, h).wait_recv()
            own[j, h] = (
                own[j, h].astype(jnp.float32) + core_got[j, h].astype(jnp.float32)
            ).astype(jnp.bfloat16)
        y_copy(j).start()

    def add_y(j):
        y_copy(j).wait_recv()
        return own[j, half].astype(jnp.float32) + y_got[j].astype(jnp.float32)

    add_core(0)

    def step(j, carry):
        add_core(j)
        own[j - 1, half] = add_y(j - 1).astype(jnp.bfloat16)
        wide_copy(j - 1).start()
        return carry

    lax.fori_loop(1, wide, step, 0)
    total = add_y(wide - 1)

    def collect(j, acc):
        wide_copy(j).wait_recv()
        return acc + wide_got[j].astype(jnp.float32)

    total = lax.fori_loop(0, wide - 1, collect, total)
    mixed = (base_ref[...].astype(jnp.float32) + total).astype(jnp.bfloat16)
    out_ref[...] = jnp.dot(back_ref[...], mixed, preferred_element_type=jnp.float32).astype(
        jnp.bfloat16
    )

    def finish(j, carry):
        core_copy(j, 0).wait_send()
        core_copy(j, 1).wait_send()
        y_copy(j).wait_send()
        return carry

    lax.fori_loop(0, wide, finish, 0)

    def finish_wide(j, carry):
        wide_copy(j).wait_send()
        return carry

    lax.fori_loop(0, wide - 1, finish_wide, 0)


def scatter_call(low, base, back, wide):
    rows, cols = base.shape
    dma = pltpu.SemaphoreType.DMA
    vmem = pl.BlockSpec(memory_space=pltpu.VMEM)
    scratch = 6 * wide * rows * cols * 2
    return pl.pallas_call(
        functools.partial(scatter_kernel, wide),
        out_shape=jax.ShapeDtypeStruct((rows, cols), jnp.bfloat16),
        in_specs=[pl.BlockSpec(memory_space=pl.ANY), vmem, vmem],
        out_specs=vmem,
        scratch_shapes=[
            pltpu.VMEM((wide, 2, rows, cols), jnp.bfloat16),
            pltpu.VMEM((wide, 2, rows, cols), jnp.bfloat16),
            pltpu.VMEM((wide, rows, cols), jnp.bfloat16),
            pltpu.VMEM((wide, rows, cols), jnp.bfloat16),
            dma((2, wide)),
            dma((2, wide)),
            dma((2, wide)),
            dma((wide,)),
            dma((wide,)),
            dma((wide,)),
            dma((wide,)),
        ],
        compiler_params=pltpu.CompilerParams(
            collective_id=1, has_side_effects=True, vmem_limit_bytes=scratch + 12 * 2**20
        ),
    )(low, base, back)


def local(
    attn_heads,
    w_out,
    residual,
    norm_gain,
    route_ids,
    route_weight,
    row_order,
    slot_expert,
    w_in,
    w_down,
):
    rows = residual.shape[0]
    wide = lax.axis_size("wide")
    me = lax.axis_index("wide")
    width_local = residual.shape[1]
    slot_local, _, hid, width = w_in.shape
    pair = rows // wide

    target = row_order // rows
    earlier = jnp.arange(rows)[None, :] < jnp.arange(rows)[:, None]
    rank = jnp.sum((target[:, None] == target[None, :]) & earlier, axis=1, dtype=jnp.int32)
    packed = target * pair + rank
    perm = packed[None, :] == jnp.arange(rows, dtype=jnp.int32)[:, None]
    order = perm.astype(jnp.bfloat16)
    meta = jnp.concatenate(
        [
            route_ids.astype(jnp.float32),
            route_weight,
            (row_order % rows).astype(jnp.float32)[:, None],
        ],
        axis=1,
    )
    meta = jnp.sum(jnp.where(perm[:, :, None], meta[None], 0.0), axis=1)
    metas = lax.all_gather(meta, "wide", axis=0, tiled=True)
    attn = jnp.dot(order, attn_heads, preferred_element_type=jnp.float32).astype(jnp.bfloat16)
    res = jnp.dot(order, residual, preferred_element_type=jnp.float32)

    def regroup(x):
        return (
            x.reshape(wide, wide, pair, x.shape[1])
            .transpose(1, 0, 2, 3)
            .reshape(wide * rows, x.shape[1])
        )

    gathered = regroup(gather_call(attn, w_out, res, wide))
    metas = regroup(metas)
    whole = gathered.astype(jnp.float32)
    mean_sq = jnp.mean(whole * whole, axis=1, keepdims=True)
    normed = (whole * lax.rsqrt(mean_sq + 1e-06) * norm_gain).astype(jnp.bfloat16)

    slots = slot_expert.shape[0]
    before = jnp.arange(slots)[None, :] < jnp.arange(slots)[:, None]
    repeated = jnp.any((slot_expert[:, None] == slot_expert[None, :]) & before, axis=1)
    used = jnp.where(repeated, -1, slot_expert)
    mine = lax.dynamic_slice_in_dim(used, me * slot_local, slot_local).astype(jnp.float32)
    ids, weights, places = metas[:, :4], metas[:, 4:8], metas[:, 8]
    coef = jnp.sum(
        jnp.where(ids[:, :, None] == mine[None, None, :], weights[:, :, None], 0.0), axis=1
    )

    gate = jnp.einsum("rd,shd->rsh", normed, w_in[:, 0], preferred_element_type=jnp.float32)
    up = jnp.einsum("rd,shd->rsh", normed, w_in[:, 1], preferred_element_type=jnp.float32)
    act = (jax.nn.relu(gate) * up * coef[:, :, None]).astype(jnp.bfloat16)
    lowered = jnp.dot(
        act.reshape(wide * rows, slot_local * hid),
        w_down.reshape(slot_local * hid, width),
        preferred_element_type=jnp.float32,
    ).astype(jnp.bfloat16)
    base = lax.dynamic_slice(
        gathered,
        (me * rows, lax.axis_index("narrow") * width_local),
        (rows, width_local),
    )
    place = lax.dynamic_slice_in_dim(places, me * rows, rows).astype(jnp.int32)
    back = (place[None, :] == jnp.arange(rows, dtype=jnp.int32)[:, None]).astype(jnp.bfloat16)
    return scatter_call(lowered, base, back, wide)


def solution(mesh):
    placed = (
        P("wide", "narrow"),
        P("narrow", None),
        P("wide", "narrow"),
        P(),
        P("wide", None),
        P("wide", None),
        P("wide"),
        P(),
        P("wide", None, "narrow", None),
        P("wide", "narrow", None),
    )
    return jax.shard_map(
        local, mesh=mesh, in_specs=placed, out_specs=P("wide", "narrow"), check_vma=False
    )
```

```python
import functools

import jax
import jax.numpy as jnp
from jax import lax
from jax.experimental import pallas as pl
from jax.experimental.pallas import tpu as pltpu
from jax.sharding import PartitionSpec as P

MESH = pl.DeviceIdType.MESH
NARROW = 4


def remote(src, dst, send_sem, recv_sem, wide_index, narrow_index):
    return pltpu.make_async_remote_copy(
        src_ref=src,
        dst_ref=dst,
        send_sem=send_sem,
        recv_sem=recv_sem,
        device_id=(wide_index, narrow_index),
        device_id_type=MESH,
    )


def greet(wide, me, col, others):
    barrier = pltpu.get_barrier_semaphore()

    def hello(j, carry):
        pl.semaphore_signal(
            barrier, inc=1, device_id=(lax.rem(me + j, wide), col), device_id_type=MESH
        )
        return carry

    lax.fori_loop(1, wide, hello, 0)
    for other in others:
        pl.semaphore_signal(barrier, inc=1, device_id=(me, other), device_id_type=MESH)
    pl.semaphore_wait(barrier, wide - 1 + len(others))


def gather_kernel(
    wide,
    attn_ref,
    w_ref,
    res_ref,
    meta_ref,
    out_ref,
    metas_ref,
    parts,
    got,
    mine,
    sum_send,
    sum_recv,
    local_sem,
    wide_send,
    wide_recv,
    y_send,
    y_recv,
    core_send,
    core_recv,
    meta_send,
    meta_recv,
):
    me, col = lax.axis_index("wide"), lax.axis_index("narrow")
    half, core = col // 2, lax.rem(col, 2)
    y_col = (1 - half) * 2 + core
    core_col = half * 2 + 1 - core
    rows, cols = res_ref.shape
    greet(wide, me, col, [lax.rem(col + k, NARROW) for k in range(1, NARROW)])

    def meta_copy(j):
        return remote(
            meta_ref,
            metas_ref.at[me],
            meta_send.at[j],
            meta_recv.at[j],
            lax.rem(me + j, wide),
            col,
        )

    def send_meta(j, carry):
        meta_copy(j).start()
        return carry

    metas_ref[me] = meta_ref[...]
    lax.fori_loop(1, wide, send_meta, 0)

    for p in range(NARROW):
        parts[p] = jnp.dot(
            attn_ref[...], w_ref[:, p * cols : (p + 1) * cols], preferred_element_type=jnp.float32
        ).astype(jnp.bfloat16)
    sums = []
    for k in range(1, NARROW):
        other = lax.rem(col + k, NARROW)
        copy = remote(
            parts.at[other], got.at[k - 1], sum_send.at[k - 1], sum_recv.at[k - 1], me, other
        )
        copy.start()
        sums.append(copy)
    total = res_ref[...] + parts[col].astype(jnp.float32)
    for k, copy in enumerate(sums):
        copy.wait_recv()
        total += got[k].astype(jnp.float32)
    mine[...] = total.astype(jnp.bfloat16)

    def block(source, column):
        return out_ref.at[
            pl.ds(pl.multiple_of(source * rows, rows), rows),
            pl.ds(pl.multiple_of(column * cols, cols), cols),
        ]

    def wide_copy(j):
        return remote(
            mine, block(me, col), wide_send.at[j], wide_recv.at[j], lax.rem(me + j, wide), col
        )

    def y_copy(j):
        b = block(lax.rem(me - j + wide, wide), col)
        return remote(b, b, y_send.at[j], y_recv.at[j], me, y_col)

    def core_copy(j, h):
        b = block(lax.rem(me - j + wide, wide), y_col if h else col)
        return remote(b, b, core_send.at[h, j], core_recv.at[h, j], me, core_col)

    def send_wide(j, carry):
        wide_copy(j).start()
        return carry

    lax.fori_loop(1, wide, send_wide, 0)
    keep = pltpu.make_async_copy(mine, block(me, col), local_sem)
    keep.start()
    keep.wait()
    y_copy(0).start()
    core_copy(0, 0).start()

    def forward(j, carry):
        wide_copy(j).wait_recv()
        y_copy(j).start()
        core_copy(j, 0).start()
        y_copy(j - 1).wait_recv()
        core_copy(j - 1, 1).start()
        return carry

    lax.fori_loop(1, wide, forward, 0)
    y_copy(wide - 1).wait_recv()
    core_copy(wide - 1, 1).start()

    def finish(j, carry):
        core_copy(j, 0).wait()
        core_copy(j, 1).wait()
        y_copy(j).wait_send()
        return carry

    lax.fori_loop(0, wide, finish, 0)

    def finish_wide(j, carry):
        wide_copy(j).wait_send()
        meta_copy(j).wait()
        return carry

    lax.fori_loop(1, wide, finish_wide, 0)
    for copy in sums:
        copy.wait_send()


def gather_call(attn, w_out, res, meta, wide):
    rows, cols = res.shape
    dma = pltpu.SemaphoreType.DMA
    vmem = pl.BlockSpec(memory_space=pltpu.VMEM)
    return pl.pallas_call(
        functools.partial(gather_kernel, wide),
        out_shape=(
            jax.ShapeDtypeStruct((wide * rows, NARROW * cols), jnp.bfloat16),
            jax.ShapeDtypeStruct((wide,) + meta.shape, jnp.float32),
        ),
        in_specs=[vmem] * 4,
        out_specs=(pl.BlockSpec(memory_space=pl.ANY), vmem),
        scratch_shapes=[
            pltpu.VMEM((NARROW, rows, cols), jnp.bfloat16),
            pltpu.VMEM((NARROW - 1, rows, cols), jnp.bfloat16),
            pltpu.VMEM((rows, cols), jnp.bfloat16),
            dma((NARROW - 1,)),
            dma((NARROW - 1,)),
            dma,
            dma((wide,)),
            dma((wide,)),
            dma((wide,)),
            dma((wide,)),
            dma((2, wide)),
            dma((2, wide)),
            dma((wide,)),
            dma((wide,)),
        ],
        compiler_params=pltpu.CompilerParams(
            collective_id=0, has_side_effects=True, vmem_limit_bytes=32 * 2**20
        ),
    )(attn, w_out, res, meta)


def scatter_kernel(
    wide,
    low_ref,
    base_ref,
    back_ref,
    out_ref,
    own,
    core_got,
    y_got,
    wide_got,
    local_sem,
    core_send,
    core_recv,
    y_send,
    y_recv,
    wide_send,
    wide_recv,
):
    me, col = lax.axis_index("wide"), lax.axis_index("narrow")
    half, core = col // 2, lax.rem(col, 2)
    y_col = (1 - half) * 2 + core
    core_col = half * 2 + 1 - core
    rows, cols = base_ref.shape
    greet(wide, me, col, [y_col, core_col])

    def target(j):
        return lax.rem(me + 1 + j, wide)

    def block(j, column):
        return low_ref.at[
            pl.ds(pl.multiple_of(target(j) * rows, rows), rows),
            pl.ds(pl.multiple_of(column * cols, cols), cols),
        ]

    def core_copy(j, h):
        return remote(
            block(j, h * 2 + 1 - core),
            core_got.at[j, h],
            core_send.at[h, j],
            core_recv.at[h, j],
            me,
            core_col,
        )

    def load(j, h):
        return pltpu.make_async_copy(block(j, h * 2 + core), own.at[j, h], local_sem.at[h, j])

    def y_copy(j):
        return remote(own.at[j, 1 - half], y_got.at[j], y_send.at[j], y_recv.at[j], me, y_col)

    def wide_copy(j):
        return remote(
            own.at[j, half], wide_got.at[j], wide_send.at[j], wide_recv.at[j], target(j), col
        )

    def begin(j, carry):
        for h in range(2):
            core_copy(j, h).start()
            load(j, h).start()
        return carry

    lax.fori_loop(0, wide, begin, 0)

    def add_core(j):
        for h in range(2):
            load(j, h).wait()
            core_copy(j, h).wait_recv()
            own[j, h] = (
                own[j, h].astype(jnp.float32) + core_got[j, h].astype(jnp.float32)
            ).astype(jnp.bfloat16)
        y_copy(j).start()

    def add_y(j):
        y_copy(j).wait_recv()
        return own[j, half].astype(jnp.float32) + y_got[j].astype(jnp.float32)

    add_core(0)

    def step(j, carry):
        add_core(j)
        own[j - 1, half] = add_y(j - 1).astype(jnp.bfloat16)
        wide_copy(j - 1).start()
        return carry

    lax.fori_loop(1, wide, step, 0)
    total = add_y(wide - 1)

    def collect(j, acc):
        wide_copy(j).wait_recv()
        return acc + wide_got[j].astype(jnp.float32)

    total = lax.fori_loop(0, wide - 1, collect, total)
    mixed = (base_ref[...].astype(jnp.float32) + total).astype(jnp.bfloat16)
    out_ref[...] = jnp.dot(back_ref[...], mixed, preferred_element_type=jnp.float32).astype(
        jnp.bfloat16
    )

    def finish(j, carry):
        core_copy(j, 0).wait_send()
        core_copy(j, 1).wait_send()
        y_copy(j).wait_send()
        return carry

    lax.fori_loop(0, wide, finish, 0)

    def finish_wide(j, carry):
        wide_copy(j).wait_send()
        return carry

    lax.fori_loop(0, wide - 1, finish_wide, 0)


def scatter_call(low, base, back, wide):
    rows, cols = base.shape
    dma = pltpu.SemaphoreType.DMA
    vmem = pl.BlockSpec(memory_space=pltpu.VMEM)
    scratch = 6 * wide * rows * cols * 2
    return pl.pallas_call(
        functools.partial(scatter_kernel, wide),
        out_shape=jax.ShapeDtypeStruct((rows, cols), jnp.bfloat16),
        in_specs=[pl.BlockSpec(memory_space=pl.ANY), vmem, vmem],
        out_specs=vmem,
        scratch_shapes=[
            pltpu.VMEM((wide, 2, rows, cols), jnp.bfloat16),
            pltpu.VMEM((wide, 2, rows, cols), jnp.bfloat16),
            pltpu.VMEM((wide, rows, cols), jnp.bfloat16),
            pltpu.VMEM((wide, rows, cols), jnp.bfloat16),
            dma((2, wide)),
            dma((2, wide)),
            dma((2, wide)),
            dma((wide,)),
            dma((wide,)),
            dma((wide,)),
            dma((wide,)),
        ],
        compiler_params=pltpu.CompilerParams(
            collective_id=1, has_side_effects=True, vmem_limit_bytes=scratch + 12 * 2**20
        ),
    )(low, base, back)


def local(
    attn_heads,
    w_out,
    residual,
    norm_gain,
    route_ids,
    route_weight,
    row_order,
    slot_expert,
    w_in,
    w_down,
):
    rows = residual.shape[0]
    wide = lax.axis_size("wide")
    me = lax.axis_index("wide")
    width_local = residual.shape[1]
    slot_local, _, hid, width = w_in.shape
    pair = rows // wide

    target = row_order // rows
    earlier = jnp.arange(rows)[None, :] < jnp.arange(rows)[:, None]
    rank = jnp.sum((target[:, None] == target[None, :]) & earlier, axis=1, dtype=jnp.int32)
    packed = target * pair + rank
    perm = packed[None, :] == jnp.arange(rows, dtype=jnp.int32)[:, None]
    order = perm.astype(jnp.bfloat16)
    meta = jnp.concatenate(
        [
            route_ids.astype(jnp.float32),
            route_weight,
            (row_order % rows).astype(jnp.float32)[:, None],
        ],
        axis=1,
    )
    meta = jnp.sum(jnp.where(perm[:, :, None], meta[None], 0.0), axis=1)
    fields = meta.shape[1]
    meta = jnp.pad(meta.T, ((0, -fields % 8), (0, 0)))
    attn = jnp.dot(order, attn_heads, preferred_element_type=jnp.float32).astype(jnp.bfloat16)
    res = jnp.dot(order, residual, preferred_element_type=jnp.float32)

    def regroup(x):
        return (
            x.reshape(wide, wide, pair, x.shape[1])
            .transpose(1, 0, 2, 3)
            .reshape(wide * rows, x.shape[1])
        )

    gathered, metas = gather_call(attn, w_out, res, meta, wide)
    gathered = regroup(gathered)
    metas = regroup(metas[:, :fields].transpose(0, 2, 1).reshape(wide * rows, fields))
    whole = gathered.astype(jnp.float32)
    mean_sq = jnp.mean(whole * whole, axis=1, keepdims=True)
    normed = (whole * lax.rsqrt(mean_sq + 1e-06) * norm_gain).astype(jnp.bfloat16)

    slots = slot_expert.shape[0]
    before = jnp.arange(slots)[None, :] < jnp.arange(slots)[:, None]
    repeated = jnp.any((slot_expert[:, None] == slot_expert[None, :]) & before, axis=1)
    used = jnp.where(repeated, -1, slot_expert)
    mine = lax.dynamic_slice_in_dim(used, me * slot_local, slot_local).astype(jnp.float32)
    ids, weights, places = metas[:, :4], metas[:, 4:8], metas[:, 8]
    coef = jnp.sum(
        jnp.where(ids[:, :, None] == mine[None, None, :], weights[:, :, None], 0.0), axis=1
    )

    gate = jnp.einsum("rd,shd->rsh", normed, w_in[:, 0], preferred_element_type=jnp.float32)
    up = jnp.einsum("rd,shd->rsh", normed, w_in[:, 1], preferred_element_type=jnp.float32)
    act = (jax.nn.relu(gate) * up * coef[:, :, None]).astype(jnp.bfloat16)
    lowered = jnp.dot(
        act.reshape(wide * rows, slot_local * hid),
        w_down.reshape(slot_local * hid, width),
        preferred_element_type=jnp.float32,
    ).astype(jnp.bfloat16)
    base = lax.dynamic_slice(
        gathered,
        (me * rows, lax.axis_index("narrow") * width_local),
        (rows, width_local),
    )
    place = lax.dynamic_slice_in_dim(places, me * rows, rows).astype(jnp.int32)
    back = (place[None, :] == jnp.arange(rows, dtype=jnp.int32)[:, None]).astype(jnp.bfloat16)
    return scatter_call(lowered, base, back, wide)


def solution(mesh):
    placed = (
        P("wide", "narrow"),
        P("narrow", None),
        P("wide", "narrow"),
        P(),
        P("wide", None),
        P("wide", None),
        P("wide"),
        P(),
        P("wide", None, "narrow", None),
        P("wide", "narrow", None),
    )
    return jax.shard_map(
        local, mesh=mesh, in_specs=placed, out_specs=P("wide", "narrow"), check_vma=False
    )
```

```python
import functools

import jax
import jax.numpy as jnp
from jax import lax
from jax.experimental import pallas as pl
from jax.experimental.pallas import tpu as pltpu
from jax.sharding import PartitionSpec as P

MESH = pl.DeviceIdType.MESH
NARROW = 4


def remote(src, dst, send_sem, recv_sem, wide_index, narrow_index):
    return pltpu.make_async_remote_copy(
        src_ref=src,
        dst_ref=dst,
        send_sem=send_sem,
        recv_sem=recv_sem,
        device_id=(wide_index, narrow_index),
        device_id_type=MESH,
    )


def partner(me, j, wide):
    out, bit = 0, 1
    while bit < wide:
        out = out + lax.rem(me // bit + j // bit, 2) * bit
        bit *= 2
    return out


def greet(wide, me, col, others):
    barrier = pltpu.get_barrier_semaphore()

    def hello(j, carry):
        pl.semaphore_signal(
            barrier, inc=1, device_id=(lax.rem(me + j, wide), col), device_id_type=MESH
        )
        return carry

    lax.fori_loop(1, wide, hello, 0)
    for other in others:
        pl.semaphore_signal(barrier, inc=1, device_id=(me, other), device_id_type=MESH)
    pl.semaphore_wait(barrier, wide - 1 + len(others))


def gather_kernel(
    wide,
    attn_ref,
    w_ref,
    res_ref,
    meta_ref,
    out_ref,
    metas_ref,
    parts,
    got,
    mine,
    sum_send,
    sum_recv,
    local_sem,
    wide_send,
    wide_recv,
    y_send,
    y_recv,
    core_send,
    core_recv,
    meta_send,
    meta_recv,
):
    me, col = lax.axis_index("wide"), lax.axis_index("narrow")
    half, core = col // 2, lax.rem(col, 2)
    y_col = (1 - half) * 2 + core
    core_col = half * 2 + 1 - core
    rows, cols = res_ref.shape
    greet(wide, me, col, [lax.rem(col + k, NARROW) for k in range(1, NARROW)])

    def meta_copy(j):
        return remote(
            meta_ref,
            metas_ref.at[me],
            meta_send.at[j],
            meta_recv.at[j],
            lax.rem(me + j, wide),
            col,
        )

    def send_meta(j, carry):
        meta_copy(j).start()
        return carry

    metas_ref[me] = meta_ref[...]
    lax.fori_loop(1, wide, send_meta, 0)

    for p in range(NARROW):
        parts[p] = jnp.dot(
            attn_ref[...], w_ref[:, p * cols : (p + 1) * cols], preferred_element_type=jnp.float32
        ).astype(jnp.bfloat16)
    sums = []
    for k in range(1, NARROW):
        other = lax.rem(col + k, NARROW)
        copy = remote(
            parts.at[other], got.at[k - 1], sum_send.at[k - 1], sum_recv.at[k - 1], me, other
        )
        copy.start()
        sums.append(copy)
    total = res_ref[...] + parts[col].astype(jnp.float32)
    for k, copy in enumerate(sums):
        copy.wait_recv()
        total += got[k].astype(jnp.float32)
    mine[...] = total.astype(jnp.bfloat16)

    def block(source, column):
        return out_ref.at[
            pl.ds(pl.multiple_of(source * rows, rows), rows),
            pl.ds(pl.multiple_of(column * cols, cols), cols),
        ]

    def wide_copy(j):
        return remote(
            mine, block(me, col), wide_send.at[j], wide_recv.at[j], partner(me, j, wide), col
        )

    def y_copy(j):
        b = block(partner(me, j, wide), col)
        return remote(b, b, y_send.at[j], y_recv.at[j], me, y_col)

    def core_copy(j, h):
        b = block(partner(me, j, wide), y_col if h else col)
        return remote(b, b, core_send.at[h, j], core_recv.at[h, j], me, core_col)

    def send_wide(j, carry):
        wide_copy(j).start()
        return carry

    lax.fori_loop(1, wide, send_wide, 0)
    keep = pltpu.make_async_copy(mine, block(me, col), local_sem)
    keep.start()
    keep.wait()
    y_copy(0).start()
    core_copy(0, 0).start()

    def forward(j, carry):
        wide_copy(j).wait_recv()
        y_copy(j).start()
        core_copy(j, 0).start()
        y_copy(j - 1).wait_recv()
        core_copy(j - 1, 1).start()
        return carry

    lax.fori_loop(1, wide, forward, 0)
    y_copy(wide - 1).wait_recv()
    core_copy(wide - 1, 1).start()

    def finish(j, carry):
        core_copy(j, 0).wait()
        core_copy(j, 1).wait()
        y_copy(j).wait_send()
        return carry

    lax.fori_loop(0, wide, finish, 0)

    def finish_wide(j, carry):
        wide_copy(j).wait_send()
        meta_copy(j).wait()
        return carry

    lax.fori_loop(1, wide, finish_wide, 0)
    for copy in sums:
        copy.wait_send()


def gather_call(attn, w_out, res, meta, wide):
    rows, cols = res.shape
    dma = pltpu.SemaphoreType.DMA
    vmem = pl.BlockSpec(memory_space=pltpu.VMEM)
    return pl.pallas_call(
        functools.partial(gather_kernel, wide),
        out_shape=(
            jax.ShapeDtypeStruct((wide * rows, NARROW * cols), jnp.bfloat16),
            jax.ShapeDtypeStruct((wide,) + meta.shape, jnp.float32),
        ),
        in_specs=[vmem] * 4,
        out_specs=(pl.BlockSpec(memory_space=pl.ANY), vmem),
        scratch_shapes=[
            pltpu.VMEM((NARROW, rows, cols), jnp.bfloat16),
            pltpu.VMEM((NARROW - 1, rows, cols), jnp.bfloat16),
            pltpu.VMEM((rows, cols), jnp.bfloat16),
            dma((NARROW - 1,)),
            dma((NARROW - 1,)),
            dma,
            dma((wide,)),
            dma((wide,)),
            dma((wide,)),
            dma((wide,)),
            dma((2, wide)),
            dma((2, wide)),
            dma((wide,)),
            dma((wide,)),
        ],
        compiler_params=pltpu.CompilerParams(
            collective_id=0, has_side_effects=True, vmem_limit_bytes=32 * 2**20
        ),
    )(attn, w_out, res, meta)


def scatter_kernel(
    wide,
    low_ref,
    base_ref,
    back_ref,
    out_ref,
    own,
    core_got,
    y_got,
    wide_got,
    local_sem,
    core_send,
    core_recv,
    y_send,
    y_recv,
    wide_send,
    wide_recv,
):
    me, col = lax.axis_index("wide"), lax.axis_index("narrow")
    half, core = col // 2, lax.rem(col, 2)
    y_col = (1 - half) * 2 + core
    core_col = half * 2 + 1 - core
    rows, cols = base_ref.shape
    greet(wide, me, col, [y_col, core_col])

    def target(j):
        return partner(me, wide - 1 - j, wide)

    def block(j, column):
        return low_ref.at[
            pl.ds(pl.multiple_of(target(j) * rows, rows), rows),
            pl.ds(pl.multiple_of(column * cols, cols), cols),
        ]

    def core_copy(j, h):
        return remote(
            block(j, h * 2 + 1 - core),
            core_got.at[j, h],
            core_send.at[h, j],
            core_recv.at[h, j],
            me,
            core_col,
        )

    def load(j, h):
        return pltpu.make_async_copy(block(j, h * 2 + core), own.at[j, h], local_sem.at[h, j])

    def y_copy(j):
        return remote(own.at[j, 1 - half], y_got.at[j], y_send.at[j], y_recv.at[j], me, y_col)

    def wide_copy(j):
        return remote(
            own.at[j, half], wide_got.at[j], wide_send.at[j], wide_recv.at[j], target(j), col
        )

    def begin(j, carry):
        for h in range(2):
            core_copy(j, h).start()
            load(j, h).start()
        return carry

    lax.fori_loop(0, wide, begin, 0)

    def add_core(j):
        for h in range(2):
            load(j, h).wait()
            core_copy(j, h).wait_recv()
            own[j, h] = (
                own[j, h].astype(jnp.float32) + core_got[j, h].astype(jnp.float32)
            ).astype(jnp.bfloat16)
        y_copy(j).start()

    def add_y(j):
        y_copy(j).wait_recv()
        return own[j, half].astype(jnp.float32) + y_got[j].astype(jnp.float32)

    add_core(0)

    def step(j, carry):
        add_core(j)
        own[j - 1, half] = add_y(j - 1).astype(jnp.bfloat16)
        wide_copy(j - 1).start()
        return carry

    lax.fori_loop(1, wide, step, 0)
    total = add_y(wide - 1)

    def collect(j, acc):
        wide_copy(j).wait_recv()
        return acc + wide_got[j].astype(jnp.float32)

    total = lax.fori_loop(0, wide - 1, collect, total)
    mixed = (base_ref[...].astype(jnp.float32) + total).astype(jnp.bfloat16)
    out_ref[...] = jnp.dot(back_ref[...], mixed, preferred_element_type=jnp.float32).astype(
        jnp.bfloat16
    )

    def finish(j, carry):
        core_copy(j, 0).wait_send()
        core_copy(j, 1).wait_send()
        y_copy(j).wait_send()
        return carry

    lax.fori_loop(0, wide, finish, 0)

    def finish_wide(j, carry):
        wide_copy(j).wait_send()
        return carry

    lax.fori_loop(0, wide - 1, finish_wide, 0)


def scatter_call(low, base, back, wide):
    rows, cols = base.shape
    dma = pltpu.SemaphoreType.DMA
    vmem = pl.BlockSpec(memory_space=pltpu.VMEM)
    scratch = 6 * wide * rows * cols * 2
    return pl.pallas_call(
        functools.partial(scatter_kernel, wide),
        out_shape=jax.ShapeDtypeStruct((rows, cols), jnp.bfloat16),
        in_specs=[pl.BlockSpec(memory_space=pl.ANY), vmem, vmem],
        out_specs=vmem,
        scratch_shapes=[
            pltpu.VMEM((wide, 2, rows, cols), jnp.bfloat16),
            pltpu.VMEM((wide, 2, rows, cols), jnp.bfloat16),
            pltpu.VMEM((wide, rows, cols), jnp.bfloat16),
            pltpu.VMEM((wide, rows, cols), jnp.bfloat16),
            dma((2, wide)),
            dma((2, wide)),
            dma((2, wide)),
            dma((wide,)),
            dma((wide,)),
            dma((wide,)),
            dma((wide,)),
        ],
        compiler_params=pltpu.CompilerParams(
            collective_id=1, has_side_effects=True, vmem_limit_bytes=scratch + 12 * 2**20
        ),
    )(low, base, back)


def local(
    attn_heads,
    w_out,
    residual,
    norm_gain,
    route_ids,
    route_weight,
    row_order,
    slot_expert,
    w_in,
    w_down,
):
    rows = residual.shape[0]
    wide = lax.axis_size("wide")
    me = lax.axis_index("wide")
    width_local = residual.shape[1]
    slot_local, _, hid, width = w_in.shape
    pair = rows // wide

    target = row_order // rows
    earlier = jnp.arange(rows)[None, :] < jnp.arange(rows)[:, None]
    rank = jnp.sum((target[:, None] == target[None, :]) & earlier, axis=1, dtype=jnp.int32)
    packed = target * pair + rank
    perm = packed[None, :] == jnp.arange(rows, dtype=jnp.int32)[:, None]
    order = perm.astype(jnp.bfloat16)
    meta = jnp.concatenate(
        [
            route_ids.astype(jnp.float32),
            route_weight,
            (row_order % rows).astype(jnp.float32)[:, None],
        ],
        axis=1,
    )
    meta = jnp.sum(jnp.where(perm[:, :, None], meta[None], 0.0), axis=1)
    fields = meta.shape[1]
    meta = jnp.pad(meta.T, ((0, -fields % 8), (0, 0)))
    attn = jnp.dot(order, attn_heads, preferred_element_type=jnp.float32).astype(jnp.bfloat16)
    res = jnp.dot(order, residual, preferred_element_type=jnp.float32)

    def regroup(x):
        return (
            x.reshape(wide, wide, pair, x.shape[1])
            .transpose(1, 0, 2, 3)
            .reshape(wide * rows, x.shape[1])
        )

    gathered, metas = gather_call(attn, w_out, res, meta, wide)
    gathered = regroup(gathered)
    metas = regroup(metas[:, :fields].transpose(0, 2, 1).reshape(wide * rows, fields))
    whole = gathered.astype(jnp.float32)
    mean_sq = jnp.mean(whole * whole, axis=1, keepdims=True)
    normed = (whole * lax.rsqrt(mean_sq + 1e-06) * norm_gain).astype(jnp.bfloat16)

    slots = slot_expert.shape[0]
    before = jnp.arange(slots)[None, :] < jnp.arange(slots)[:, None]
    repeated = jnp.any((slot_expert[:, None] == slot_expert[None, :]) & before, axis=1)
    used = jnp.where(repeated, -1, slot_expert)
    mine = lax.dynamic_slice_in_dim(used, me * slot_local, slot_local).astype(jnp.float32)
    ids, weights, places = metas[:, :4], metas[:, 4:8], metas[:, 8]
    coef = jnp.sum(
        jnp.where(ids[:, :, None] == mine[None, None, :], weights[:, :, None], 0.0), axis=1
    )

    gate = jnp.einsum("rd,shd->rsh", normed, w_in[:, 0], preferred_element_type=jnp.float32)
    up = jnp.einsum("rd,shd->rsh", normed, w_in[:, 1], preferred_element_type=jnp.float32)
    act = (jax.nn.relu(gate) * up * coef[:, :, None]).astype(jnp.bfloat16)
    lowered = jnp.dot(
        act.reshape(wide * rows, slot_local * hid),
        w_down.reshape(slot_local * hid, width),
        preferred_element_type=jnp.float32,
    ).astype(jnp.bfloat16)
    base = lax.dynamic_slice(
        gathered,
        (me * rows, lax.axis_index("narrow") * width_local),
        (rows, width_local),
    )
    place = lax.dynamic_slice_in_dim(places, me * rows, rows).astype(jnp.int32)
    back = (place[None, :] == jnp.arange(rows, dtype=jnp.int32)[:, None]).astype(jnp.bfloat16)
    return scatter_call(lowered, base, back, wide)


def solution(mesh):
    placed = (
        P("wide", "narrow"),
        P("narrow", None),
        P("wide", "narrow"),
        P(),
        P("wide", None),
        P("wide", None),
        P("wide"),
        P(),
        P("wide", None, "narrow", None),
        P("wide", "narrow", None),
    )
    return jax.shard_map(
        local, mesh=mesh, in_specs=placed, out_specs=P("wide", "narrow"), check_vma=False
    )
```
